512 devices in a mesh: dp: 16 (over y, core), mp: 32 (over x, z).
Axes of the slice: x: 4, y: 8, z: 8, core: 2. Of those that a mesh axis runs over, the one named last changes fastest.
Arguments:
- grad_partials: bfloat16 [16, 224, 512, 512], P('dp', 'mp')
- owner_lists: int32 [224], replicated, may hold values from 0 to 223, as said below
- owner_offsets: int32 [33], replicated, may hold values from 0 to 224, as said below
- left_roots: bfloat16 [32, 16, 512, 512], P('mp', 'dp')
- right_roots: bfloat16 [32, 16, 512, 512], P('mp', 'dp')
Outputs:
- update: bfloat16 [224, 512, 512], P('mp', 'dp')
The draws below stay inside these ranges and needn't reach their ends.
Inputs may be any that keep to these rules, and one draw needn't show every extreme that they name: `owner_lists`: a permutation of the block numbers; no owner column owns two blocks of one mp shard (blocks j * 7 to j * 7 + 6). `owner_offsets`: begins with 0, ends with 224, never falls; every owner column owns 1 to 16 blocks, and some column exactly 16.
All inputs are finite; a program needn't handle non-finite values.
Results may differ from the reference program's by a relative error of at most 0.025.
Values may be sent and summed in bfloat16 or wider, within the bound.
A program may use at most 64 MiB of HBM per device.

```python
import math
import jax
import jax.numpy as jnp
from jax import lax

BLOCK = 512
BLK_DEV = 7
BLOCKS = 224
N_DP = 16
N_MP = 32


def ownership(key):
    key = jax.random.fold_in(key, 5)
    first_key, second_key, third_key = jax.random.split(key, 3)
    column_order = jax.random.permutation(first_key, N_MP)
    needed = N_DP - BLK_DEV
    ranks = jnp.arange(N_MP, dtype=jnp.int32)
    given = jnp.clip(needed - (ranks - 1) * (BLK_DEV - 1), 0, BLK_DEV - 1)
    ranked_counts = jnp.where(ranks == 0, N_DP, BLK_DEV - given).astype(jnp.int32)
    counts = jnp.zeros((N_MP,), jnp.int32).at[column_order].set(ranked_counts)
    offsets = jnp.concatenate([jnp.zeros((1,), jnp.int32), jnp.cumsum(counts).astype(jnp.int32)])
    rotation = jax.random.randint(second_key, (), 0, BLOCKS)
    shard_order = jax.random.permutation(third_key, N_MP)
    sequence = (jnp.arange(BLOCKS, dtype=jnp.int32) + rotation) % BLOCKS
    levels = sequence // N_MP
    shards = shard_order[sequence % N_MP]
    lists = (shards * BLK_DEV + levels).astype(jnp.int32)
    return (lists, offsets)


def draw_owner_lists(key, part):
    lists, offsets = ownership(key)
    return lists


def draw_owner_offsets(key, part):
    lists, offsets = ownership(key)
    return offsets


def draw_grad_partials(key, part):
    key = jax.random.fold_in(key, 11)
    row_key, col_key, noise_key = jax.random.split(key, 3)
    row_scale = jnp.exp(jax.random.uniform(row_key, (BLOCKS, BLOCK, 1)) * math.log(10.0))
    col_scale = jnp.exp(jax.random.uniform(col_key, (BLOCKS, 1, BLOCK)) * math.log(10.0))
    rising = (1.0 + 2.0 * jnp.arange(BLOCKS, dtype=jnp.float32) / max(BLOCKS - 1, 1)).reshape(BLOCKS, 1, 1)
    row_place = (jnp.arange(BLOCK, dtype=jnp.float32) / max(BLOCK - 1, 1)).reshape(1, BLOCK, 1)
    noise = jax.random.normal(noise_key, (N_DP, BLOCKS, BLOCK, BLOCK))
    factor = 0.1
    row_rise = 1.0 + 2.0 * row_place
    return (factor * rising * row_rise * row_scale * col_scale * noise).astype(jnp.bfloat16)


def symmetric_root(key, diag_low, diag_high):
    off_key, diag_key = jax.random.split(key)
    spread = 0.9 / math.sqrt(BLOCK)
    offdiag = jax.random.uniform(off_key, (N_MP, N_DP, BLOCK, BLOCK), minval=-spread, maxval=spread)
    offdiag = 0.5 * (offdiag + jnp.swapaxes(offdiag, -1, -2))
    diagonal = jax.random.uniform(diag_key, (N_MP, N_DP, BLOCK, 1), minval=diag_low, maxval=diag_high)
    identity = (jnp.arange(BLOCK)[:, None] == jnp.arange(BLOCK)[None, :]).astype(jnp.float32)
    return (offdiag + diagonal * identity).astype(jnp.bfloat16)


def draw_left_roots(key, part):
    key = jax.random.fold_in(key, 21)
    return symmetric_root(key, 1.0, 2.0)


def draw_right_roots(key, part):
    key = jax.random.fold_in(key, 22)
    return symmetric_root(key, 1.0, 2.0)


def setup_inputs(seed: int = 0) -> dict:
    key_list = jax.random.split(jax.random.key(seed), 6)
    grad_partials = draw_grad_partials(jax.random.fold_in(key_list[5], 71), 0)
    owner_lists = draw_owner_lists(jax.random.fold_in(key_list[5], 71), 0)
    owner_offsets = draw_owner_offsets(jax.random.fold_in(key_list[5], 71), 0)
    left_roots = draw_left_roots(jax.random.fold_in(key_list[5], 71), 0)
    right_roots = draw_right_roots(jax.random.fold_in(key_list[5], 71), 0)
    return {"grad_partials": grad_partials, "owner_lists": owner_lists, "owner_offsets": owner_offsets, "left_roots": left_roots, "right_roots": right_roots}


epsilon = 1e-06
max_rms = 1.0

def reference(grad_partials, owner_lists, owner_offsets, left_roots, right_roots):
    grad = grad_partials[0].astype(jnp.float32)
    for replica in range(1, N_DP):
        grad = grad + grad_partials[replica].astype(jnp.float32)
    grad_b = grad.astype(jnp.bfloat16)
    grad_sq = grad_b.astype(jnp.float32)
    square_total = jnp.sum(grad_sq * grad_sq)
    clip_factor = max_rms / jnp.sqrt(square_total / (BLOCKS * BLOCK * BLOCK) + epsilon)
    positions = jnp.arange(BLOCKS, dtype=jnp.int32)
    owner_column = lax.optimization_barrier(jnp.sum((owner_offsets[1:][None, :] <= positions[:, None]).astype(jnp.int32), axis=1)).astype(jnp.int32)
    owner_slot = (positions - owner_offsets[owner_column]).astype(jnp.int32)

    def precondition(position):
        block_id = owner_lists[position]
        whole_block = grad_b[block_id]
        left_factor = left_roots[owner_column[position], owner_slot[position]]
        right_factor = right_roots[owner_column[position], owner_slot[position]]
        right_prod = jnp.dot(whole_block, right_factor, preferred_element_type=jnp.float32).astype(jnp.bfloat16)
        precond = jnp.dot(left_factor, right_prod, preferred_element_type=jnp.float32)
        block_f = whole_block.astype(jnp.float32)
        graft_scale = jnp.sqrt(jnp.mean(block_f * block_f) + epsilon) / jnp.sqrt(jnp.mean(precond * precond) + epsilon)
        return (clip_factor * graft_scale * precond).astype(jnp.bfloat16)
    results = lax.map(precondition, positions)
    update = jnp.zeros((BLOCKS, BLOCK, BLOCK), jnp.bfloat16).at[owner_lists].set(results)
    return update
```

```python
import functools

import jax
import jax.numpy as jnp
from jax import lax
from jax.experimental import pallas as pl
from jax.experimental.pallas import tpu as pltpu
from jax.sharding import PartitionSpec as P

MESH = pl.DeviceIdType.MESH
F32 = jnp.float32
BF16 = jnp.bfloat16

epsilon = 1e-06
max_rms = 1.0

CHUNKS = 2
NY, NX, NZ = 8, 4, 8
SLAB = 32
HALF = SLAB // 2

T_FWD = 0
T_SLOT = 32
T_RET = 48
T_HX = 80
T_MINE = 136
T_SIZE = 192


def routing_tables(owner_lists, owner_offsets, per_shard):
    blocks = owner_lists.shape[0]
    mp = lax.axis_index("mp")
    x, z = mp // NZ, mp % NZ
    positions = jnp.arange(blocks, dtype=jnp.int32)
    column_of_pos = jnp.sum(
        (owner_offsets[1:][None, :] <= positions[:, None]).astype(jnp.int32), axis=1
    )
    line = NZ * per_shard
    line_blocks = x * line + jnp.arange(line, dtype=jnp.int32)
    matches = owner_lists[None, :] == line_blocks[:, None]
    home = jnp.sum(jnp.where(matches, column_of_pos[None, :], 0), axis=1).reshape(NZ, per_shard)
    home_x, mine = home // NZ, (home % NZ == z).astype(jnp.int32)
    to_x = jnp.arange(NX, dtype=jnp.int32)
    ids = jnp.arange(per_shard, dtype=jnp.int32)
    picked = home[:, None, :] == (to_x * NZ + z)[None, :, None]
    forward = jnp.sum(jnp.where(picked, ids[None, None, :], 0), axis=2)
    start = owner_offsets[mp]
    count = owner_offsets[mp + 1] - start
    slots = jnp.arange(2 * NY, dtype=jnp.int32)
    at = (start + slots)[:, None] == positions[None, :]
    block = jnp.sum(jnp.where(at, owner_lists[None, :], 0), axis=1)
    shard = block // per_shard
    delta = (shard % NZ - z + NZ) % NZ
    place = jnp.where(
        delta == 0, 0, jnp.where(delta < 4, 2 * delta - 1, jnp.where(delta == 4, 7, 2 * (NZ - delta)))
    )
    slot_place = (shard // NZ) * NZ + place
    shards_all = jnp.arange(NX * NZ, dtype=jnp.int32)
    owned = (shard[None, :] == shards_all[:, None]) & (slots < count)[None, :]
    back = jnp.sum(jnp.where(owned, slots[None, :], 0), axis=1)
    parts = [forward.reshape(-1), slot_place, back, home_x.reshape(-1), mine.reshape(-1)]
    return jnp.concatenate(parts).astype(jnp.int32)


def kernel(
    nc,
    cells,
    tab,
    g,
    left,
    right,
    out,
    own,
    other,
    red,
    slab,
    zin,
    zfar,
    xsend,
    arrived,
    csend,
    block,
    done,
    rows,
    esend,
    ein,
    emix,
    ered,
    lv,
    rv,
    acc,
    sq,
    sq_d,
    sq_x,
    sq_z,
    sem_in,
    core_s,
    core_r,
    ra_s,
    ra_r,
    rb_s,
    rb_r,
    xb_s,
    xb_r,
    c_s,
    c_r,
    d_s,
    d_r,
    xe_s,
    xe_r,
    re_s,
    re_r,
    qd_s,
    qd_r,
    qx_s,
    qx_r,
    qz_s,
    qz_r,
):
    per_shard = g.shape[0]
    width = g.shape[-1] // nc
    edge = g.shape[-1]
    area = edge * edge
    n_dp = 2 * NY
    dp = lax.axis_index("dp")
    mp = lax.axis_index("mp")
    y, core = dp // 2, dp % 2
    x, z = mp // NZ, mp % NZ
    mate = y * 2 + (1 - core)
    y_to = [((y + NY - 1) % NY) * 2 + core, ((y + 1) % NY) * 2 + core]
    z_to = [x * NZ + (z + NZ - 1) % NZ, x * NZ + (z + 1) % NZ]

    def x_to(j):
        return ((x + j) % NX) * NZ + z

    def cols(c):
        return pl.ds(c * width, width)

    sent = []

    def send(src, dst, ss, rs, dev):
        copy = pltpu.make_async_remote_copy(
            src_ref=src, dst_ref=dst, send_sem=ss, recv_sem=rs, device_id=dev, device_id_type=MESH
        )
        copy.start()
        sent.append(copy)

    def received(dst, rs, ss):
        pltpu.make_async_remote_copy(
            src_ref=dst, dst_ref=dst, send_sem=ss, recv_sem=rs, device_id={"dp": mate}, device_id_type=MESH
        ).wait_recv()

    loads = []
    for c in range(nc):
        load = pltpu.make_async_copy(g.at[:, :, core, :, cols(c)], own.at[c], sem_in.at[c])
        load.start()
        loads.append(load)
    load_r = pltpu.make_async_copy(right, rv, sem_in.at[nc])
    load_r.start()
    load_l = pltpu.make_async_copy(left, lv, sem_in.at[nc + 1])
    load_l.start()

    barrier = pltpu.get_barrier_semaphore()

    @pl.loop(1, n_dp)
    def _(o):
        pl.semaphore_signal(barrier, inc=1, device_id={"dp": (dp + o) % n_dp}, device_id_type=MESH)

    @pl.loop(1, NX)
    def _(o):
        pl.semaphore_signal(barrier, inc=1, device_id={"mp": ((x + o) % NX) * NZ + z}, device_id_type=MESH)

    @pl.loop(1, NZ)
    def _(o):
        pl.semaphore_signal(barrier, inc=1, device_id={"mp": x * NZ + (z + o) % NZ}, device_id_type=MESH)

    pl.semaphore_wait(barrier, n_dp + NX + NZ - 3)

    for c in range(nc):
        send(g.at[:, :, 1 - core, :, cols(c)], other.at[c], core_s.at[c], core_r.at[c], {"dp": mate})

    lo, hi = pl.ds(0, HALF), pl.ds(HALF, HALF)
    part = [lo, hi]

    def pair(c, t, r):
        return own[c, :, t, r].astype(F32) + other[c, :, t, r].astype(F32)

    everything = pl.ds(0, SLAB)

    def a0(c):
        loads[c].wait()
        received(other.at[c], core_r.at[c], core_s.at[c])
        t = (y + 4) % NY
        own[c, :, t] = pair(c, t, everything).astype(BF16)
        for way in range(2):
            send(
                own.at[c, :, t, part[way]],
                red.at[c, way, 0, :, part[way]],
                ra_s.at[c, way, 0],
                ra_r.at[c, way, 0],
                {"dp": y_to[way]},
            )

    def a_mid(c, s):
        for way in range(2):
            t = (y + NY + (s - 4 if way == 0 else 4 - s)) % NY
            if s == 1:
                here, rest = part[way], part[1 - way]
                received(red.at[c, way, 0, :, here], ra_r.at[c, way, 0], ra_s.at[c, way, 0])
                own[c, :, t, here] = (pair(c, t, here) + red[c, way, 0, :, here].astype(F32)).astype(BF16)
                own[c, :, t, rest] = pair(c, t, rest).astype(BF16)
            else:
                received(red.at[c, way, s - 1], ra_r.at[c, way, s - 1], ra_s.at[c, way, s - 1])
                own[c, :, t] = (pair(c, t, everything) + red[c, way, s - 1].astype(F32)).astype(BF16)
            send(own.at[c, :, t], red.at[c, way, s], ra_s.at[c, way, s], ra_r.at[c, way, s], {"dp": y_to[way]})

    def squares(v):
        v = (v * v).reshape(-1, 8, v.shape[-1])
        v = jnp.sum(v, axis=0)
        return sum(v[:, i * 128 : (i + 1) * 128] for i in range(v.shape[-1] // 128))

    def a4(c):
        total = pair(c, y, everything)
        for way in range(2):
            received(red.at[c, way, 3], ra_r.at[c, way, 3], ra_s.at[c, way, 3])
            total += red[c, way, 3].astype(F32)
        total = total.astype(BF16)
        slab[c] = total
        for way in range(2):
            send(slab.at[c], zin[c][way][0], rb_s.at[c, way, 0], rb_r.at[c, way, 0], {"mp": z_to[way]})
        part_sq = squares(total.astype(F32))
        sq[0] = part_sq if c == 0 else sq[0] + part_sq
        pick(c, slab.at[c], z, 0)

    def pick(c, src, zs, place):
        for j in range(NX):
            chosen = src[tab[T_FWD + zs * NX + (x + j) % NX]]
            if j == 0:
                arrived[c][x * NZ + place] = chosen
            else:
                xsend[c, j - 1, place] = chosen

    groups = [(0, 3), (3, 2), (5, 2), (7, 1)]

    def x_send(c, n):
        first, size = groups[n]
        for j in range(1, NX):
            send(
                xsend.at[c, j - 1, pl.ds(first, size)],
                arrived[c].at[pl.ds(x * NZ + first, size)],
                xb_s.at[c, j - 1, n],
                xb_r.at[c, j - 1, n],
                {"mp": x_to(j)},
            )

    def b_mid(c, s):
        for way in range(2):
            received(zin[c][way][s - 1], rb_r.at[c, way, s - 1], rb_s.at[c, way, s - 1])
            if s < 3:
                src, dst = zin[c][way][s - 1], zin[c][way][s]
            else:
                src, dst = zin[c][way][2].at[:, part[way]], zfar[c].at[:, part[way]]
            send(src, dst, rb_s.at[c, way, s], rb_r.at[c, way, s], {"mp": z_to[way]})
        for way in range(2):
            zs = (z + s) % NZ if way == 0 else (z + NZ - s) % NZ
            pick(c, zin[c][way][s - 1], zs, 2 * s - 1 + way)
        x_send(c, s - 1)

    def b4(c):
        for way in range(2):
            received(zfar[c].at[:, part[way]], rb_r.at[c, way, 3], rb_s.at[c, way, 3])
        pick(c, zfar[c], (z + 4) % NZ, 7)
        x_send(c, 3)

    def c0(c):
        for j in range(1, NX):
            for n in range(4):
                first, size = groups[n]
                came = arrived[c].at[pl.ds(((x + NX - j) % NX) * NZ + first, size)]
                received(came, xb_r.at[c, j - 1, n], xb_s.at[c, j - 1, n])
        block[c, dp] = arrived[c][tab[T_SLOT + dp]]

        @pl.loop(1, n_dp)
        def _(o):
            k = (dp + o) % n_dp
            csend[c, k] = arrived[c][tab[T_SLOT + k]]
            pltpu.make_async_remote_copy(
                src_ref=csend.at[c, k],
                dst_ref=block.at[c, dp],
                send_sem=c_s.at[c, o],
                recv_sem=c_r.at[c, o],
                device_id={"dp": k},
                device_id_type=MESH,
            ).start()

    def dp_received(buf, c, rs, ss):
        @pl.loop(1, n_dp)
        def _(o):
            received(buf.at[(dp + n_dp - o) % n_dp], rs.at[c, o], ss.at[c, o])

    def c1(c):
        dp_received(block.at[c], c, c_r, c_s)
        if c == 0:
            load_r.wait()
        rows_c = block[c].reshape(edge, width)
        product = jnp.dot(rows_c, rv[cols(c), :], preferred_element_type=F32)
        acc[...] = product if c == 0 else acc[...] + product
        part_sq = squares(rows_c.astype(F32))
        sq[3] = part_sq if c == 0 else sq[3] + part_sq

    def q0():
        @pl.loop(1, n_dp)
        def _(o):
            pltpu.make_async_remote_copy(
                src_ref=sq.at[0],
                dst_ref=sq_d.at[o],
                send_sem=qd_s.at[o],
                recv_sem=qd_r.at[o],
                device_id={"dp": (dp + o) % n_dp},
                device_id_type=MESH,
            ).start()

    def q1():
        total = sq[0]
        for o in range(1, n_dp):
            received(sq_d.at[o], qd_r.at[o], qd_s.at[o])
            total += sq_d[o]
        sq[1] = total
        for j in range(1, NX):
            send(sq.at[1], sq_x.at[j], qx_s.at[j], qx_r.at[j], {"mp": x_to(j)})

    def q2():
        total = sq[1]
        for j in range(1, NX):
            received(sq_x.at[j], qx_r.at[j], qx_s.at[j])
            total += sq_x[j]
        sq[2] = total
        for o in range(1, NZ):
            send(sq.at[2], sq_z.at[o], qz_s.at[o], qz_r.at[o], {"mp": x * NZ + (z + o) % NZ})

    def q3():
        total = sq[2]
        for o in range(1, NZ):
            received(sq_z.at[o], qz_r.at[o], qz_s.at[o])
            total += sq_z[o]
        return jnp.sum(total, keepdims=True)

    stages = [
        a0,
        functools.partial(a_mid, s=1),
        functools.partial(a_mid, s=2),
        functools.partial(a_mid, s=3),
        a4,
        functools.partial(b_mid, s=1),
        functools.partial(b_mid, s=2),
        functools.partial(b_mid, s=3),
        b4,
        c0,
        c1,
    ]
    for slot in range(len(stages) + nc - 1):
        for c in range(nc):
            n = slot - c
            if 0 <= n < len(stages):
                stages[n](c)
            if c == nc - 1:
                if n == 4:
                    q0()
                if n == 6:
                    q1()
                if n == 8:
                    q2()

    load_l.wait()
    acc[...] = jnp.dot(lv[...], acc[...].astype(BF16), preferred_element_type=F32)
    precond_sq = sum(squares(acc[:, cols(c)]) for c in range(nc))
    graft = jnp.sqrt(jnp.sum(sq[3], keepdims=True) / area + epsilon) / jnp.sqrt(
        jnp.sum(precond_sq, keepdims=True) / area + epsilon
    )
    clip = max_rms / jnp.sqrt(q3() / cells + epsilon)
    scale = clip * graft

    def d0(c):
        done[c] = (scale * acc[:, cols(c)]).astype(BF16).reshape(n_dp, SLAB, width)
        rows[c][dp] = done[c, dp]

        @pl.loop(1, n_dp)
        def _(o):
            k = (dp + o) % n_dp
            pltpu.make_async_remote_copy(
                src_ref=done.at[c, k],
                dst_ref=rows[c].at[dp],
                send_sem=d_s.at[c, o],
                recv_sem=d_r.at[c, o],
                device_id={"dp": k},
                device_id_type=MESH,
            ).start()

    def e0(c):
        dp_received(rows[c], c, d_r, d_s)
        for j in [1, 2, 3, 0]:
            for zs in range(NZ):
                chosen = rows[c][tab[T_RET + ((x + j) % NX) * NZ + zs]]
                if j == 0:
                    ein[c][x, zs] = chosen
                else:
                    esend[c, j - 1, zs] = chosen
            if j:
                send(esend.at[c, j - 1], ein[c].at[x], xe_s.at[c, j - 1], xe_r.at[c, j - 1], {"mp": x_to(j)})

    def merge(c, t, i, r, incoming):
        at = t * per_shard + i
        return jnp.where(tab[T_MINE + at] == 1, ein[c][tab[T_HX + at], t, r], incoming)

    zero_half = jnp.zeros((HALF, width), BF16)
    zero = jnp.zeros((SLAB, width), BF16)

    def e1(c):
        for j in range(1, NX):
            received(ein[c].at[(x + NX - j) % NX], xe_r.at[c, j - 1], xe_s.at[c, j - 1])
        t = (z + 4) % NZ
        for i in range(per_shard):
            emix[c, t, i] = merge(c, t, i, everything, zero)
        for way in range(2):
            send(
                emix.at[c, t, :, part[way]],
                ered.at[c, way, 0, :, part[way]],
                re_s.at[c, way, 0],
                re_r.at[c, way, 0],
                {"mp": z_to[way]},
            )

    def e_mid(c, s):
        for way in range(2):
            t = (z + NZ + (s - 4 if way == 0 else 4 - s)) % NZ
            if s == 1:
                here, rest = part[way], part[1 - way]
                received(ered.at[c, way, 0, :, here], re_r.at[c, way, 0], re_s.at[c, way, 0])
                for i in range(per_shard):
                    emix[c, t, i, here] = merge(c, t, i, here, ered[c, way, 0, i, here])
                    emix[c, t, i, rest] = merge(c, t, i, rest, zero_half)
            else:
                received(ered.at[c, way, s - 1], re_r.at[c, way, s - 1], re_s.at[c, way, s - 1])
                for i in range(per_shard):
                    emix[c, t, i] = merge(c, t, i, everything, ered[c, way, s - 1, i])
            send(emix.at[c, t], ered.at[c, way, s], re_s.at[c, way, s], re_r.at[c, way, s], {"mp": z_to[way]})

    def e5(c):
        for way in range(2):
            received(ered.at[c, way, 3], re_r.at[c, way, 3], re_s.at[c, way, 3])
        for i in range(per_shard):
            out[i, :, cols(c)] = merge(c, z, i, everything, ered[c, 0, 3, i] + ered[c, 1, 3, i])

    for c in range(nc):
        d0(c)
    stages = [
        e0,
        e1,
        functools.partial(e_mid, s=1),
        functools.partial(e_mid, s=2),
        functools.partial(e_mid, s=3),
        e5,
    ]
    for slot in range(len(stages) + nc - 1):
        for c in range(nc):
            if 0 <= slot - c < len(stages):
                stages[slot - c](c)

    for copy in sent:
        copy.wait_send()

    @pl.loop(1, n_dp)
    def _(o):
        for c in range(nc):
            k = (dp + o) % n_dp
            for src, ss, rs in ((csend, c_s, c_r), (done, d_s, d_r)):
                pltpu.make_async_remote_copy(
                    src_ref=src.at[c, k],
                    dst_ref=src.at[c, k],
                    send_sem=ss.at[c, o],
                    recv_sem=rs.at[c, o],
                    device_id={"dp": k},
                    device_id_type=MESH,
                ).wait_send()
        pltpu.make_async_remote_copy(
            src_ref=sq.at[0],
            dst_ref=sq_d.at[o],
            send_sem=qd_s.at[o],
            recv_sem=qd_r.at[o],
            device_id={"dp": (dp + o) % n_dp},
            device_id_type=MESH,
        ).wait_send()


def shards(grad_partials, owner_lists, owner_offsets, left_roots, right_roots):
    _, per_shard, edge, _ = grad_partials.shape
    nc = CHUNKS
    width = edge // nc
    n_dp = 2 * NY
    tables = routing_tables(owner_lists, owner_offsets, per_shard)
    g = grad_partials.reshape(per_shard, NY, 2, SLAB, edge)
    dma = pltpu.SemaphoreType.DMA

    def both(*shape):
        return [dma(shape), dma(shape)]

    anywhere = pl.BlockSpec(memory_space=pl.ANY)
    return pl.pallas_call(
        functools.partial(kernel, nc, owner_lists.shape[0] * edge * edge),
        out_shape=jax.ShapeDtypeStruct((per_shard, SLAB, edge), BF16),
        in_specs=[pl.BlockSpec(memory_space=pltpu.SMEM), anywhere, anywhere, anywhere],
        out_specs=pl.BlockSpec(memory_space=pltpu.VMEM),
        scratch_shapes=[
            pltpu.VMEM((nc, per_shard, NY, SLAB, width), BF16),
            pltpu.VMEM((nc, per_shard, NY, SLAB, width), BF16),
            pltpu.VMEM((nc, 2, 4, per_shard, SLAB, width), BF16),
            pltpu.VMEM((nc, per_shard, SLAB, width), BF16),
            [[[pltpu.VMEM((per_shard, SLAB, width), BF16)] * 3] * 2] * nc,
            [pltpu.VMEM((per_shard, SLAB, width), BF16)] * nc,
            pltpu.VMEM((nc, NX - 1, NZ, SLAB, width), BF16),
            [pltpu.VMEM((NX * NZ, SLAB, width), BF16)] * nc,
            pltpu.VMEM((nc, n_dp, SLAB, width), BF16),
            pltpu.VMEM((nc, n_dp, SLAB, width), BF16),
            pltpu.VMEM((nc, n_dp, SLAB, width), BF16),
            [pltpu.VMEM((n_dp, SLAB, width), BF16)] * nc,
            pltpu.VMEM((nc, NX - 1, NZ, SLAB, width), BF16),
            [pltpu.VMEM((NX, NZ, SLAB, width), BF16)] * nc,
            pltpu.VMEM((nc, NZ, per_shard, SLAB, width), BF16),
            pltpu.VMEM((nc, 2, 4, per_shard, SLAB, width), BF16),
            pltpu.VMEM((edge, edge), BF16),
            pltpu.VMEM((edge, edge), BF16),
            pltpu.VMEM((edge, edge), F32),
            pltpu.VMEM((4, 8, 128), F32),
            pltpu.VMEM((n_dp, 8, 128), F32),
            pltpu.VMEM((NX, 8, 128), F32),
            pltpu.VMEM((NZ, 8, 128), F32),
            dma((nc + 2,)),
            *both(nc),
            *both(nc, 2, 4),
            *both(nc, 2, 4),
            *both(nc, NX - 1, 4),
            *both(nc, n_dp),
            *both(nc, n_dp),
            *both(nc, NX - 1),
            *both(nc, 2, 4),
            *both(n_dp),
            *both(NX),
            *both(NZ),
        ],
        compiler_params=pltpu.CompilerParams(
            collective_id=0, has_side_effects=True, vmem_limit_bytes=48 * 1024 * 1024
        ),
    )(tables, g, left_roots[0, 0], right_roots[0, 0])


def solution(mesh):
    return jax.shard_map(
        shards,
        mesh=mesh,
        in_specs=(
            P("dp", "mp", None, None),
            P(),
            P(),
            P("mp", "dp", None, None),
            P("mp", "dp", None, None),
        ),
        out_specs=P("mp", "dp", None),
        check_vma=False,
    )
```

```python
import functools

import jax
import jax.numpy as jnp
from jax import lax
from jax.experimental import pallas as pl
from jax.experimental.pallas import tpu as pltpu
from jax.sharding import PartitionSpec as P

MESH = pl.DeviceIdType.MESH
F32 = jnp.float32
BF16 = jnp.bfloat16

epsilon = 1e-06
max_rms = 1.0

CHUNKS = 4
NY, NX, NZ = 8, 4, 8
SLAB = 32
HALF = SLAB // 2

S_CORE, S_HALF, S_RING, S_B, S_C, S_D, S_E, S_QD, S_QX, S_QZ = range(10)


def kernel(
    nc,
    cells,
    lists,
    lists_row,
    offsets,
    g,
    left,
    right,
    out,
    own,
    other,
    red,
    slab,
    bsend,
    arrived,
    csend,
    block,
    done,
    rows,
    esend,
    home_in,
    lv,
    rv,
    acc,
    sq,
    sq_d,
    sq_x,
    sq_z,
    to_column,
    slot_shard,
    back_slot,
    home,
    sem_in,
    core_r,
    ring_r,
    send_sem,
    recv_sem,
):
    per_shard = g.shape[0]
    width = g.shape[-1] // nc
    edge = g.shape[-1]
    area = edge * edge
    n_dp, n_mp = 2 * NY, NX * NZ
    R_B, R_C, R_D, R_E, R_Q = 0, nc, 2 * nc, 3 * nc, 4 * nc
    dp = lax.axis_index("dp")
    mp = lax.axis_index("mp")
    y, core = dp // 2, dp % 2
    x, z = mp // NZ, mp % NZ
    mate = {"dp": y * 2 + (1 - core)}
    y_to = [{"dp": ((y + NY - 1) % NY) * 2 + core}, {"dp": ((y + 1) % NY) * 2 + core}]

    def dp_to(o):
        return {"dp": (dp + o) % n_dp}

    def mp_to(o):
        return {"mp": (mp + o) % n_mp}

    def x_to(o):
        return {"mp": ((x + o) % NX) * NZ + z}

    def z_to(o):
        return {"mp": x * NZ + (z + o) % NZ}

    def cols(c):
        return pl.ds(c * width, width)

    def copy(src, dst, ss, rs, dev):
        return pltpu.make_async_remote_copy(
            src_ref=src, dst_ref=dst, send_sem=ss, recv_sem=rs, device_id=dev, device_id_type=MESH
        )

    def send(*args):
        copy(*args).start()

    def received(dst, rs):
        copy(dst, dst, send_sem.at[0], rs, mate).wait_recv()

    def all_sent(src, ss):
        copy(src, src, ss, recv_sem.at[0], mate).wait_send()

    loads = []
    for c in range(nc):
        load = pltpu.make_async_copy(g.at[:, :, core, :, cols(c)], own.at[c], sem_in.at[c])
        load.start()
        loads.append(load)
    load_r = pltpu.make_async_copy(right, rv, sem_in.at[nc])
    load_r.start()
    load_l = pltpu.make_async_copy(left, lv, sem_in.at[nc + 1])
    load_l.start()

    barrier = pltpu.get_barrier_semaphore()

    @pl.loop(1, n_dp)
    def _(o):
        pl.semaphore_signal(barrier, inc=1, device_id=dp_to(o), device_id_type=MESH)

    @pl.loop(1, n_mp)
    def _(o):
        pl.semaphore_signal(barrier, inc=1, device_id=mp_to(o), device_id_type=MESH)

    pl.semaphore_wait(barrier, n_dp + n_mp - 2)

    for d in [4, 5, 3, 6, 2, 7, 1, 0]:
        t = (y + d) % NY
        for c in range(nc):
            send(g.at[:, t, 1 - core, :, cols(c)], other.at[c, :, t], send_sem.at[S_CORE], core_r.at[d], mate)

    everything = pl.ds(0, SLAB)
    part = [pl.ds(0, HALF), pl.ds(HALF, HALF)]

    def mated(c, d):
        t = (y + d) % NY
        if c == 0:
            received(other.at[:, :, t], core_r.at[d])
        return t

    def pair(c, t, r):
        return own[c, :, t, r].astype(F32) + other[c, :, t, r].astype(F32)

    def a0(c):
        loads[c].wait()
        t = mated(c, 4)
        own[c, :, t] = pair(c, t, everything).astype(BF16)
        for way in range(2):
            send(
                own.at[c, :, t, part[way]],
                red.at[c, way, 0, :, part[way]],
                send_sem.at[S_HALF],
                ring_r.at[c, way, 0],
                y_to[way],
            )

    def a_mid(c, s):
        for way in range(2):
            t = mated(c, 4 + s if way == 0 else 4 - s)
            if s == 1:
                here, rest = part[way], part[1 - way]
                received(red.at[c, way, 0, :, here], ring_r.at[c, way, 0])
                own[c, :, t, here] = (pair(c, t, here) + red[c, way, 0, :, here].astype(F32)).astype(BF16)
                own[c, :, t, rest] = pair(c, t, rest).astype(BF16)
            else:
                received(red.at[c, way, s - 1], ring_r.at[c, way, s - 1])
                own[c, :, t] = (pair(c, t, everything) + red[c, way, s - 1].astype(F32)).astype(BF16)
            send(own.at[c, :, t], red.at[c, way, s], send_sem.at[S_RING], ring_r.at[c, way, s], y_to[way])

    def squares(v):
        v = (v * v).reshape(-1, 8, v.shape[-1])
        v = jnp.sum(v, axis=0)
        return sum(v[:, i * 128 : (i + 1) * 128] for i in range(v.shape[-1] // 128))

    def a4(c):
        total = pair(c, mated(c, 0), everything)
        for way in range(2):
            received(red.at[c, way, 3], ring_r.at[c, way, 3])
            total += red[c, way, 3].astype(F32)
        total = total.astype(BF16)
        slab[c] = total
        b0(c)
        part_sq = squares(total.astype(F32))
        sq[0] = part_sq if c == 0 else sq[0] + part_sq

    def tables():
        blocks = lists.shape[0]
        position = lax.broadcasted_iota(jnp.int32, (1, blocks), 1)
        column = jnp.zeros((1, blocks), jnp.int32)
        for m in range(1, n_mp + 1):
            column += jnp.where(offsets[m] <= position, 1, 0)
        homes = []
        for i in range(per_shard):
            mine = jnp.where(lists_row[...] == mp * per_shard + i, column, 0)
            homes.append(jnp.minimum(jnp.sum(mine), n_mp - 1))
            home[i] = homes[i]
        start = offsets[mp]
        count = offsets[mp + 1] - start
        shard = []
        for k in range(n_dp):
            shard.append(lists[jnp.minimum(start + k, blocks - 1)] // per_shard)
            slot_shard[k] = shard[k]

        @pl.loop(0, n_mp)
        def _(m):
            chosen = jnp.int32(0)
            for i in range(per_shard):
                chosen = jnp.where(homes[i] == m, i, chosen)
            to_column[m] = chosen
            slot = jnp.int32(0)
            for k in range(n_dp):
                slot = jnp.where((shard[k] == m) & (k < count), k, slot)
            back_slot[m] = slot

    def b0(c):
        @pl.loop(1, n_mp)
        def _(o):
            bsend[c, o] = slab[c, to_column[(mp + o) % n_mp]]
            send(bsend.at[c, o], arrived[c].at[mp], send_sem.at[S_B], recv_sem.at[R_B + c], mp_to(o))

        arrived[c][mp] = slab[c, to_column[mp]]

    def c0(c):
        received(arrived[c].at[pl.ds(1, n_mp - 1)], recv_sem.at[R_B + c])

        @pl.loop(1, n_dp)
        def _(o):
            csend[c, o] = arrived[c][slot_shard[(dp + o) % n_dp]]
            send(csend.at[c, o], block.at[c, dp], send_sem.at[S_C], recv_sem.at[R_C + c], dp_to(o))

        block[c, dp] = arrived[c][slot_shard[dp]]

    def c1(c):
        received(block.at[c, pl.ds(1, n_dp - 1)], recv_sem.at[R_C + c])
        rows_c = block[c].reshape(edge, width)
        product = jnp.dot(rows_c, rv[cols(c), :], preferred_element_type=F32)
        acc[...] = product if c == 0 else acc[...] + product
        part_sq = squares(rows_c.astype(F32))
        sq[3] = part_sq if c == 0 else sq[3] + part_sq

    def q0():
        @pl.loop(1, n_dp)
        def _(o):
            send(sq.at[0], sq_d.at[o], send_sem.at[S_QD], recv_sem.at[R_Q], dp_to(o))

    def q1():
        total = sq[0]
        received(sq_d.at[pl.ds(1, n_dp - 1)], recv_sem.at[R_Q])
        for o in range(1, n_dp):
            total += sq_d[o]
        sq[1] = total
        for o in range(1, NX):
            send(sq.at[1], sq_x.at[o], send_sem.at[S_QX], recv_sem.at[R_Q + 1], x_to(o))

    def q2():
        total = sq[1]
        received(sq_x.at[pl.ds(1, NX - 1)], recv_sem.at[R_Q + 1])
        for o in range(1, NX):
            total += sq_x[o]
        sq[2] = total
        for o in range(1, NZ):
            send(sq.at[2], sq_z.at[o], send_sem.at[S_QZ], recv_sem.at[R_Q + 2], z_to(o))

    def q3():
        total = sq[2]
        received(sq_z.at[pl.ds(1, NZ - 1)], recv_sem.at[R_Q + 2])
        for o in range(1, NZ):
            total += sq_z[o]
        return jnp.sum(total, keepdims=True)

    for c in range(nc):
        a0(c)
    tables()
    for s in (1, 2, 3):
        for c in range(nc):
            a_mid(c, s)
    for c in range(nc):
        a4(c)
    q0()
    q1()
    for c in range(nc):
        c0(c)
        if c == 0:
            q2()
            load_r.wait()
    for c in range(nc):
        c1(c)

    load_l.wait()
    acc[...] = jnp.dot(lv[...], acc[...].astype(BF16), preferred_element_type=F32)
    precond_sq = sum(squares(acc[:, cols(c)]) for c in range(nc))
    graft = jnp.sqrt(jnp.sum(sq[3], keepdims=True) / area + epsilon) / jnp.sqrt(
        jnp.sum(precond_sq, keepdims=True) / area + epsilon
    )
    clip = max_rms / jnp.sqrt(q3() / cells + epsilon)
    scale = clip * graft

    def d0(c):
        done[c] = (scale * acc[:, cols(c)]).astype(BF16).reshape(n_dp, SLAB, width)

        @pl.loop(1, n_dp)
        def _(o):
            send(done.at[c, (dp + o) % n_dp], rows[c].at[dp], send_sem.at[S_D], recv_sem.at[R_D + c], dp_to(o))

        rows[c][dp] = done[c, dp]

    def e0(c):
        received(rows[c].at[pl.ds(1, n_dp - 1)], recv_sem.at[R_D + c])

        @pl.loop(1, n_mp)
        def _(o):
            esend[c, o] = rows[c][back_slot[(mp + o) % n_mp]]
            send(esend.at[c, o], home_in[c].at[mp], send_sem.at[S_E], recv_sem.at[R_E + c], mp_to(o))

        home_in[c][mp] = rows[c][back_slot[mp]]

    def e1(c):
        received(home_in[c].at[pl.ds(1, n_mp - 1)], recv_sem.at[R_E + c])
        for i in range(per_shard):
            out[i, :, cols(c)] = home_in[c][home[i]]

    for c in range(nc):
        d0(c)
    for c in range(nc):
        e0(c)
    for c in range(nc):
        e1(c)

    all_sent(other, send_sem.at[S_CORE])
    all_sent(red.at[:, 0, 0], send_sem.at[S_HALF])
    all_sent(red.at[:, :, pl.ds(1, 3)], send_sem.at[S_RING])
    all_sent(bsend.at[:, pl.ds(1, n_mp - 1)], send_sem.at[S_B])
    all_sent(csend.at[:, pl.ds(1, n_dp - 1)], send_sem.at[S_C])
    all_sent(csend.at[:, pl.ds(1, n_dp - 1)], send_sem.at[S_D])
    all_sent(esend.at[:, pl.ds(1, n_mp - 1)], send_sem.at[S_E])
    all_sent(sq_d.at[pl.ds(1, n_dp - 1)], send_sem.at[S_QD])
    all_sent(sq_x.at[pl.ds(1, NX - 1)], send_sem.at[S_QX])
    all_sent(sq_z.at[pl.ds(1, NZ - 1)], send_sem.at[S_QZ])


def shards(grad_partials, owner_lists, owner_offsets, left_roots, right_roots):
    _, per_shard, edge, _ = grad_partials.shape
    blocks = owner_lists.shape[0]
    nc = CHUNKS
    width = edge // nc
    n_dp, n_mp = 2 * NY, NX * NZ
    g = grad_partials.reshape(per_shard, NY, 2, SLAB, edge)
    dma = pltpu.SemaphoreType.DMA

    small = pl.BlockSpec(memory_space=pltpu.SMEM)
    vmem = pl.BlockSpec(memory_space=pltpu.VMEM)
    large = pl.BlockSpec(memory_space=pltpu.HBM)
    return pl.pallas_call(
        functools.partial(kernel, nc, blocks * edge * edge),
        out_shape=jax.ShapeDtypeStruct((per_shard, SLAB, edge), BF16),
        in_specs=[small, vmem, small, large, large, large],
        out_specs=vmem,
        scratch_shapes=[
            pltpu.VMEM((nc, per_shard, NY, SLAB, width), BF16),
            pltpu.VMEM((nc, per_shard, NY, SLAB, width), BF16),
            pltpu.VMEM((nc, 2, 4, per_shard, SLAB, width), BF16),
            pltpu.VMEM((nc, per_shard, SLAB, width), BF16),
            pltpu.VMEM((nc, n_mp, SLAB, width), BF16),
            [pltpu.VMEM((n_mp, SLAB, width), BF16)] * nc,
            pltpu.VMEM((nc, n_dp, SLAB, width), BF16),
            pltpu.VMEM((nc, n_dp, SLAB, width), BF16),
            pltpu.VMEM((nc, n_dp, SLAB, width), BF16),
            [pltpu.VMEM((n_dp, SLAB, width), BF16)] * nc,
            pltpu.VMEM((nc, n_mp, SLAB, width), BF16),
            [pltpu.VMEM((n_mp, SLAB, width), BF16)] * nc,
            pltpu.VMEM((edge, edge), BF16),
            pltpu.VMEM((edge, edge), BF16),
            pltpu.VMEM((edge, edge), F32),
            pltpu.VMEM((4, 8, 128), F32),
            pltpu.VMEM((n_dp, 8, 128), F32),
            pltpu.VMEM((NX, 8, 128), F32),
            pltpu.VMEM((NZ, 8, 128), F32),
            pltpu.SMEM((n_mp,), jnp.int32),
            pltpu.SMEM((n_dp,), jnp.int32),
            pltpu.SMEM((n_mp,), jnp.int32),
            pltpu.SMEM((per_shard,), jnp.int32),
            dma((nc + 2,)),
            dma((NY,)),
            dma((nc, 2, 4)),
            dma((10,)),
            dma((4 * nc + 3,)),
        ],
        compiler_params=pltpu.CompilerParams(
            collective_id=0, has_side_effects=True, vmem_limit_bytes=63 * 1024 * 1024
        ),
    )(owner_lists, owner_lists.reshape(1, blocks), owner_offsets, g, left_roots[0, 0], right_roots[0, 0])


def solution(mesh):
    return jax.shard_map(
        shards,
        mesh=mesh,
        in_specs=(
            P("dp", "mp", None, None),
            P(),
            P(),
            P("mp", "dp", None, None),
            P("mp", "dp", None, None),
        ),
        out_specs=P("mp", "dp", None),
        check_vma=False,
    )
```

```python
import functools

import jax
import jax.numpy as jnp
from jax import lax
from jax.experimental import pallas as pl
from jax.experimental.pallas import tpu as pltpu
from jax.sharding import PartitionSpec as P

MESH = pl.DeviceIdType.MESH
F32 = jnp.float32
BF16 = jnp.bfloat16

epsilon = 1e-06
max_rms = 1.0

CHUNKS = 4
NY, NX, NZ = 8, 4, 8
SLAB = 32
ROW_PARTS = 2
LAG = 4

S_CORE, S_HALF, S_RING, S_B, S_C, S_D, S_E, S_QD, S_QX, S_QZ = range(10)


def kernel(
    nc,
    cells,
    lists,
    lists_row,
    offsets,
    g,
    left,
    right,
    out,
    own,
    other,
    red,
    slab,
    bsend,
    arrived,
    csend,
    block,
    done,
    rows,
    esend,
    home_in,
    lv,
    rv,
    acc,
    sq,
    sq_d,
    sq_x,
    sq_z,
    to_column,
    slot_shard,
    back_slot,
    home,
    sem_in,
    core_r,
    ring_r,
    send_sem,
    recv_sem,
):
    per_shard = g.shape[0]
    width = g.shape[-1] // nc
    piece_rows = SLAB // ROW_PARTS
    pieces = nc * ROW_PARTS
    edge = g.shape[-1]
    area = edge * edge
    n_dp, n_mp = 2 * NY, NX * NZ
    R_B, R_C, R_D, R_E, R_Q = 0, pieces, 2 * pieces, 3 * pieces, 4 * pieces
    dp = lax.axis_index("dp")
    mp = lax.axis_index("mp")
    y, core = dp // 2, dp % 2
    x, z = mp // NZ, mp % NZ
    mate = {"dp": y * 2 + (1 - core)}
    y_to = [{"dp": ((y + NY - 1) % NY) * 2 + core}, {"dp": ((y + 1) % NY) * 2 + core}]

    def dp_to(o):
        return {"dp": (dp + o) % n_dp}

    def mp_to(o):
        return {"mp": (mp + o) % n_mp}

    def x_to(o):
        return {"mp": ((x + o) % NX) * NZ + z}

    def z_to(o):
        return {"mp": x * NZ + (z + o) % NZ}

    def cols(c):
        return pl.ds(c * width, width)

    def of(p):
        return p // ROW_PARTS, pl.ds(p % ROW_PARTS * piece_rows, piece_rows)

    def copy(src, dst, ss, rs, dev):
        return pltpu.make_async_remote_copy(
            src_ref=src, dst_ref=dst, send_sem=ss, recv_sem=rs, device_id=dev, device_id_type=MESH
        )

    def send(*args):
        copy(*args).start()

    def received(dst, rs):
        copy(dst, dst, send_sem.at[0], rs, mate).wait_recv()

    def all_sent(src, ss):
        copy(src, src, ss, recv_sem.at[0], mate).wait_send()

    loads = []
    for c in range(nc):
        load = pltpu.make_async_copy(g.at[:, :, core, :, cols(c)], own.at[c], sem_in.at[c])
        load.start()
        loads.append(load)
    load_r = pltpu.make_async_copy(right, rv, sem_in.at[nc])
    load_r.start()
    load_l = pltpu.make_async_copy(left, lv, sem_in.at[nc + 1])
    load_l.start()

    barrier = pltpu.get_barrier_semaphore()

    @pl.loop(1, n_dp)
    def _(o):
        pl.semaphore_signal(barrier, inc=1, device_id=dp_to(o), device_id_type=MESH)

    @pl.loop(1, n_mp)
    def _(o):
        pl.semaphore_signal(barrier, inc=1, device_id=mp_to(o), device_id_type=MESH)

    pl.semaphore_wait(barrier, n_dp + n_mp - 2)

    def swap(d):
        t = (y + d) % NY
        for c in range(nc):
            send(g.at[:, t, 1 - core, :, cols(c)], other.at[c, :, t], send_sem.at[S_CORE], core_r.at[d], mate)

    def mated(p, d):
        t = (y + d) % NY
        if p == 0:
            received(other.at[:, :, t], core_r.at[d])
        return t

    def pair(c, b, t, r):
        return own[c, b, t, r].astype(F32) + other[c, b, t, r].astype(F32)

    whole = pl.ds(0, per_shard)

    def split(p):
        half = per_shard // 2 + p % 2
        return [pl.ds(0, half), pl.ds(half, per_shard - half)]

    def a0(p):
        c, r = of(p)
        if p % ROW_PARTS == 0:
            loads[c].wait()
        t = mated(p, 4)
        own[c, :, t, r] = pair(c, whole, t, r).astype(BF16)
        for way in range(2):
            b = split(p)[way]
            send(own.at[c, b, t, r], red.at[c, way, 0, b, r], send_sem.at[S_HALF], ring_r.at[p, way, 0], y_to[way])

    def a_mid(p, s):
        c, r = of(p)
        for way in range(2):
            t = mated(p, 4 + s if way == 0 else 4 - s)
            if s == 1:
                b, rest = split(p)[way], split(p)[1 - way]
                received(red.at[c, way, 0, b, r], ring_r.at[p, way, 0])
                own[c, b, t, r] = (pair(c, b, t, r) + red[c, way, 0, b, r].astype(F32)).astype(BF16)
                own[c, rest, t, r] = pair(c, rest, t, r).astype(BF16)
            else:
                received(red.at[c, way, s - 1, :, r], ring_r.at[p, way, s - 1])
                own[c, :, t, r] = (pair(c, whole, t, r) + red[c, way, s - 1, :, r].astype(F32)).astype(BF16)
            send(own.at[c, :, t, r], red.at[c, way, s, :, r], send_sem.at[S_RING], ring_r.at[p, way, s], y_to[way])

    def squares(v):
        v = (v * v).reshape(-1, 8, v.shape[-1])
        v = jnp.sum(v, axis=0)
        return sum(v[:, i * 128 : (i + 1) * 128] for i in range(v.shape[-1] // 128))

    def a4(p):
        c, r = of(p)
        total = pair(c, whole, mated(p, 0), r)
        for way in range(2):
            received(red.at[c, way, 3, :, r], ring_r.at[p, way, 3])
            total += red[c, way, 3, :, r].astype(F32)
        total = total.astype(BF16)
        slab[c, :, r] = total
        b0(p)
        part_sq = squares(total.astype(F32))
        sq[0] = part_sq if p == 0 else sq[0] + part_sq

    def tables():
        blocks = lists.shape[0]
        position = lax.broadcasted_iota(jnp.int32, (1, blocks), 1)
        column = jnp.zeros((1, blocks), jnp.int32)
        for m in range(1, n_mp + 1):
            column += jnp.where(offsets[m] <= position, 1, 0)
        homes = []
        for i in range(per_shard):
            mine = jnp.where(lists_row[...] == mp * per_shard + i, column, 0)
            homes.append(jnp.minimum(jnp.sum(mine), n_mp - 1))
            home[i] = homes[i]
        start = offsets[mp]
        count = offsets[mp + 1] - start
        shard = []
        for k in range(n_dp):
            shard.append(lists[jnp.minimum(start + k, blocks - 1)] // per_shard)
            slot_shard[k] = shard[k]

        @pl.loop(0, n_mp)
        def _(m):
            chosen = jnp.int32(0)
            for i in range(per_shard):
                chosen = jnp.where(homes[i] == m, i, chosen)
            to_column[m] = chosen
            slot = jnp.int32(0)
            for k in range(n_dp):
                slot = jnp.where((shard[k] == m) & (k < count), k, slot)
            back_slot[m] = slot

    def b0(p):
        c, r = of(p)

        @pl.loop(1, n_mp)
        def _(o):
            bsend[c, o, r] = slab[c, to_column[(mp + o) % n_mp], r]
            send(bsend.at[c, o, r], arrived[p].at[mp], send_sem.at[S_B], recv_sem.at[R_B + p], mp_to(o))

        arrived[p][mp] = slab[c, to_column[mp], r]

    def c0(p):
        c, r = of(p)
        received(arrived[p].at[pl.ds(1, n_mp - 1)], recv_sem.at[R_B + p])

        @pl.loop(1, n_dp)
        def _(o):
            csend[c, o, r] = arrived[p][slot_shard[(dp + o) % n_dp]]
            send(csend.at[c, o, r], block.at[c, dp, r], send_sem.at[S_C], recv_sem.at[R_C + p], dp_to(o))

        block[c, dp, r] = arrived[p][slot_shard[dp]]

    def c1(p):
        c, r = of(p)
        received(block.at[c, pl.ds(1, n_dp - 1), r], recv_sem.at[R_C + p])
        if (p + 1) % ROW_PARTS:
            return
        rows_c = block[c].reshape(edge, width)
        product = jnp.dot(rows_c, rv[cols(c), :], preferred_element_type=F32)
        acc[...] = product if c == 0 else acc[...] + product
        part_sq = squares(rows_c.astype(F32))
        sq[3] = part_sq if c == 0 else sq[3] + part_sq

    def q0():
        @pl.loop(1, n_dp)
        def _(o):
            send(sq.at[0], sq_d.at[o], send_sem.at[S_QD], recv_sem.at[R_Q], dp_to(o))

    def q1():
        total = sq[0]
        received(sq_d.at[pl.ds(1, n_dp - 1)], recv_sem.at[R_Q])
        for o in range(1, n_dp):
            total += sq_d[o]
        sq[1] = total
        for o in range(1, NX):
            send(sq.at[1], sq_x.at[o], send_sem.at[S_QX], recv_sem.at[R_Q + 1], x_to(o))

    def q2():
        total = sq[1]
        received(sq_x.at[pl.ds(1, NX - 1)], recv_sem.at[R_Q + 1])
        for o in range(1, NX):
            total += sq_x[o]
        sq[2] = total
        for o in range(1, NZ):
            send(sq.at[2], sq_z.at[o], send_sem.at[S_QZ], recv_sem.at[R_Q + 2], z_to(o))

    def q3():
        total = sq[2]
        received(sq_z.at[pl.ds(1, NZ - 1)], recv_sem.at[R_Q + 2])
        for o in range(1, NZ):
            total += sq_z[o]
        return jnp.sum(total, keepdims=True)

    for d in (4, 5, 3):
        swap(d)
    stages = [a0] + [functools.partial(a_mid, s=s) for s in (1, 2, 3)] + [a4]
    last = pieces - 1
    for turn in range(len(stages) + last // LAG):
        if 1 <= turn <= 3:
            for d in ((6, 2), (7, 1), (0,))[turn - 1]:
                swap(d)
        for p in range(pieces):
            n = turn - p // LAG
            if 0 <= n < len(stages):
                stages[n](p)
        if turn == 0:
            tables()
    q0()
    q1()
    for p in range(pieces):
        c0(p)
        if p == 0:
            load_r.wait()
        if p == 1:
            q2()
        if p >= 2:
            c1(p - 2)
    c1(last - 1)
    c1(last)

    load_l.wait()
    acc[...] = jnp.dot(lv[...], acc[...].astype(BF16), preferred_element_type=F32)
    precond_sq = sum(squares(acc[:, cols(c)]) for c in range(nc))
    graft = jnp.sqrt(jnp.sum(sq[3], keepdims=True) / area + epsilon) / jnp.sqrt(
        jnp.sum(precond_sq, keepdims=True) / area + epsilon
    )
    clip = max_rms / jnp.sqrt(q3() / cells + epsilon)
    scale = clip * graft

    def d0(p):
        c, r = of(p)
        if p % ROW_PARTS == 0:
            done[c] = (scale * acc[:, cols(c)]).astype(BF16).reshape(n_dp, SLAB, width)

        @pl.loop(1, n_dp)
        def _(o):
            send(done.at[c, (dp + o) % n_dp, r], rows[p].at[dp], send_sem.at[S_D], recv_sem.at[R_D + p], dp_to(o))

        rows[p][dp] = done[c, dp, r]

    def e0(p):
        c, r = of(p)
        received(rows[p].at[pl.ds(1, n_dp - 1)], recv_sem.at[R_D + p])

        @pl.loop(1, n_mp)
        def _(o):
            esend[c, o, r] = rows[p][back_slot[(mp + o) % n_mp]]
            send(esend.at[c, o, r], home_in[p].at[mp], send_sem.at[S_E], recv_sem.at[R_E + p], mp_to(o))

        home_in[p][mp] = rows[p][back_slot[mp]]

    def e1(p):
        c, r = of(p)
        received(home_in[p].at[pl.ds(1, n_mp - 1)], recv_sem.at[R_E + p])
        for i in range(per_shard):
            out[i, r, cols(c)] = home_in[p][home[i]]

    for p in range(pieces):
        d0(p)
    for p in range(pieces):
        e0(p)
    for p in range(pieces):
        e1(p)

    all_sent(other, send_sem.at[S_CORE])
    all_sent(red.at[:, 0, 0], send_sem.at[S_HALF])
    all_sent(red.at[:, :, pl.ds(1, 3)], send_sem.at[S_RING])
    all_sent(bsend.at[:, pl.ds(1, n_mp - 1)], send_sem.at[S_B])
    all_sent(csend.at[:, pl.ds(1, n_dp - 1)], send_sem.at[S_C])
    all_sent(csend.at[:, pl.ds(1, n_dp - 1)], send_sem.at[S_D])
    all_sent(esend.at[:, pl.ds(1, n_mp - 1)], send_sem.at[S_E])
    all_sent(sq_d.at[pl.ds(1, n_dp - 1)], send_sem.at[S_QD])
    all_sent(sq_x.at[pl.ds(1, NX - 1)], send_sem.at[S_QX])
    all_sent(sq_z.at[pl.ds(1, NZ - 1)], send_sem.at[S_QZ])


def shards(grad_partials, owner_lists, owner_offsets, left_roots, right_roots):
    _, per_shard, edge, _ = grad_partials.shape
    blocks = owner_lists.shape[0]
    nc = CHUNKS
    width = edge // nc
    piece_rows = SLAB // ROW_PARTS
    pieces = nc * ROW_PARTS
    n_dp, n_mp = 2 * NY, NX * NZ
    g = grad_partials.reshape(per_shard, NY, 2, SLAB, edge)
    dma = pltpu.SemaphoreType.DMA

    small = pl.BlockSpec(memory_space=pltpu.SMEM)
    vmem = pl.BlockSpec(memory_space=pltpu.VMEM)
    large = pl.BlockSpec(memory_space=pltpu.HBM)
    return pl.pallas_call(
        functools.partial(kernel, nc, blocks * edge * edge),
        out_shape=jax.ShapeDtypeStruct((per_shard, SLAB, edge), BF16),
        in_specs=[small, vmem, small, large, large, large],
        out_specs=vmem,
        scratch_shapes=[
            pltpu.VMEM((nc, per_shard, NY, SLAB, width), BF16),
            pltpu.VMEM((nc, per_shard, NY, SLAB, width), BF16),
            pltpu.VMEM((nc, 2, 4, per_shard, SLAB, width), BF16),
            pltpu.VMEM((nc, per_shard, SLAB, width), BF16),
            pltpu.VMEM((nc, n_mp, SLAB, width), BF16),
            [pltpu.VMEM((n_mp, piece_rows, width), BF16)] * pieces,
            pltpu.VMEM((nc, n_dp, SLAB, width), BF16),
            pltpu.VMEM((nc, n_dp, SLAB, width), BF16),
            pltpu.VMEM((nc, n_dp, SLAB, width), BF16),
            [pltpu.VMEM((n_dp, piece_rows, width), BF16)] * pieces,
            pltpu.VMEM((nc, n_mp, SLAB, width), BF16),
            [pltpu.VMEM((n_mp, piece_rows, width), BF16)] * pieces,
            pltpu.VMEM((edge, edge), BF16),
            pltpu.VMEM((edge, edge), BF16),
            pltpu.VMEM((edge, edge), F32),
            pltpu.VMEM((4, 8, 128), F32),
            pltpu.VMEM((n_dp, 8, 128), F32),
            pltpu.VMEM((NX, 8, 128), F32),
            pltpu.VMEM((NZ, 8, 128), F32),
            pltpu.SMEM((n_mp,), jnp.int32),
            pltpu.SMEM((n_dp,), jnp.int32),
            pltpu.SMEM((n_mp,), jnp.int32),
            pltpu.SMEM((per_shard,), jnp.int32),
            dma((nc + 2,)),
            dma((NY,)),
            dma((pieces, 2, 4)),
            dma((10,)),
            dma((4 * pieces + 3,)),
        ],
        compiler_params=pltpu.CompilerParams(
            collective_id=0, has_side_effects=True, vmem_limit_bytes=63 * 1024 * 1024
        ),
    )(owner_lists, owner_lists.reshape(1, blocks), owner_offsets, g, left_roots[0, 0], right_roots[0, 0])


def solution(mesh):
    return jax.shard_map(
        shards,
        mesh=mesh,
        in_specs=(
            P("dp", "mp", None, None),
            P(),
            P(),
            P("mp", "dp", None, None),
            P("mp", "dp", None, None),
        ),
        out_specs=P("mp", "dp", None),
        check_vma=False,
    )
```

```python
import functools

import jax
import jax.numpy as jnp
from jax import lax
from jax.experimental import pallas as pl
from jax.experimental.pallas import tpu as pltpu
from jax.sharding import PartitionSpec as P

MESH = pl.DeviceIdType.MESH
F32 = jnp.float32
BF16 = jnp.bfloat16

epsilon = 1e-06
max_rms = 1.0

CHUNKS = 4
NY, NX, NZ = 8, 4, 8
SLAB = 32
ROW_PARTS = 2
LAG = 8

S_CORE, S_HALF, S_RING, S_B, S_C, S_D, S_E, S_QD, S_QX, S_QZ = range(10)


def kernel(
    nc,
    cells,
    lists,
    lists_row,
    offsets,
    g,
    left,
    right,
    out,
    own,
    other,
    red,
    slab,
    bsend,
    arrived,
    csend,
    block,
    done,
    rows,
    esend,
    home_in,
    lv,
    rv,
    acc,
    sq,
    sq_d,
    sq_x,
    sq_z,
    to_column,
    slot_shard,
    back_slot,
    home,
    sem_in,
    core_r,
    ring_r,
    send_sem,
    recv_sem,
    entered,
):
    per_shard = g.shape[0]
    width = g.shape[-1] // nc
    piece_rows = SLAB // ROW_PARTS
    pieces = nc * ROW_PARTS
    edge = g.shape[-1]
    area = edge * edge
    n_dp, n_mp = 2 * NY, NX * NZ
    R_B, R_C, R_D, R_E, R_Q = 0, pieces, 2 * pieces, 3 * pieces, 4 * pieces
    dp = lax.axis_index("dp")
    mp = lax.axis_index("mp")
    y, core = dp // 2, dp % 2
    x, z = mp // NZ, mp % NZ
    mate = {"dp": y * 2 + (1 - core)}
    y_to = [{"dp": ((y + NY - 1) % NY) * 2 + core}, {"dp": ((y + 1) % NY) * 2 + core}]

    def dp_to(o):
        return {"dp": (dp + o) % n_dp}

    def around(k):
        return 4 + k // 2 - (k % 2) * k

    def mp_at(o):
        return ((x + NX - 1 - o % NX) % NX) * NZ + (z + around(o // NX)) % NZ

    def dp_at(o):
        return ((y + around(o // 2)) % NY) * 2 + (core + 1 - o % 2) % 2

    def x_to(o):
        return {"mp": ((x + o) % NX) * NZ + z}

    def z_to(o):
        return {"mp": x * NZ + (z + o) % NZ}

    def cols(c):
        return pl.ds(c * width, width)

    def of(p):
        return p // ROW_PARTS, pl.ds(p % ROW_PARTS * piece_rows, piece_rows)

    def copy(src, dst, ss, rs, dev):
        return pltpu.make_async_remote_copy(
            src_ref=src, dst_ref=dst, send_sem=ss, recv_sem=rs, device_id=dev, device_id_type=MESH
        )

    def send(*args):
        copy(*args).start()

    def received(dst, rs):
        copy(dst, dst, send_sem.at[0], rs, mate).wait_recv()

    def all_sent(src, ss):
        copy(src, src, ss, recv_sem.at[0], mate).wait_send()

    loads = []
    for c in range(nc):
        load = pltpu.make_async_copy(g.at[:, :, core, :, cols(c)], own.at[c], sem_in.at[c])
        load.start()
        loads.append(load)
    load_r = pltpu.make_async_copy(right, rv, sem_in.at[nc])
    load_r.start()
    load_l = pltpu.make_async_copy(left, lv, sem_in.at[nc + 1])
    load_l.start()

    barrier = pltpu.get_barrier_semaphore()
    rank = z * NX + x

    def ranked(r):
        return {"mp": (r % NX) * NZ + r // NX}

    for near in (*y_to, mate):
        pl.semaphore_signal(barrier, inc=1, device_id=near, device_id_type=MESH)

    @pl.loop(rank + 1, n_mp)
    def _(r):
        pl.semaphore_signal(barrier, inc=1, device_id=ranked(r), device_id_type=MESH)

    pl.semaphore_wait(barrier, 3 + rank)

    @pl.loop(0, rank)
    def _(r):
        pl.semaphore_signal(entered, inc=1, device_id=ranked(r), device_id_type=MESH)

    def swap(d):
        t = (y + d) % NY
        for c in range(nc):
            send(g.at[:, t, 1 - core, :, cols(c)], other.at[c, :, t], send_sem.at[S_CORE], core_r.at[d], mate)

    def mated(p, d):
        t = (y + d) % NY
        if p == 0:
            received(other.at[:, :, t], core_r.at[d])
        return t

    def pair(c, b, t, r):
        return own[c, b, t, r].astype(F32) + other[c, b, t, r].astype(F32)

    whole = pl.ds(0, per_shard)

    def split(p):
        half = per_shard // 2 + p % 2
        return [pl.ds(0, half), pl.ds(half, per_shard - half)]

    def a0(p):
        c, r = of(p)
        if p % ROW_PARTS == 0:
            loads[c].wait()
        t = mated(p, 4)
        own[c, :, t, r] = pair(c, whole, t, r).astype(BF16)
        for way in range(2):
            b = split(p)[way]
            send(own.at[c, b, t, r], red.at[c, way, 0, b, r], send_sem.at[S_HALF], ring_r.at[p, way, 0], y_to[way])

    def a_mid(p, s):
        c, r = of(p)
        for way in range(2):
            t = mated(p, 4 + s if way == 0 else 4 - s)
            if s == 1:
                b, rest = split(p)[way], split(p)[1 - way]
                received(red.at[c, way, 0, b, r], ring_r.at[p, way, 0])
                own[c, b, t, r] = (pair(c, b, t, r) + red[c, way, 0, b, r].astype(F32)).astype(BF16)
                own[c, rest, t, r] = pair(c, rest, t, r).astype(BF16)
            else:
                received(red.at[c, way, s - 1, :, r], ring_r.at[p, way, s - 1])
                own[c, :, t, r] = (pair(c, whole, t, r) + red[c, way, s - 1, :, r].astype(F32)).astype(BF16)
            send(own.at[c, :, t, r], red.at[c, way, s, :, r], send_sem.at[S_RING], ring_r.at[p, way, s], y_to[way])

    def squares(v):
        v = (v * v).reshape(-1, 8, v.shape[-1])
        v = jnp.sum(v, axis=0)
        return sum(v[:, i * 128 : (i + 1) * 128] for i in range(v.shape[-1] // 128))

    def a4(p):
        c, r = of(p)
        total = pair(c, whole, mated(p, 0), r)
        for way in range(2):
            received(red.at[c, way, 3, :, r], ring_r.at[p, way, 3])
            total += red[c, way, 3, :, r].astype(F32)
        total = total.astype(BF16)
        slab[c, :, r] = total
        b0(p)
        part_sq = squares(total.astype(F32))
        sq[0] = part_sq if p == 0 else sq[0] + part_sq

    def tables():
        blocks = lists.shape[0]
        position = lax.broadcasted_iota(jnp.int32, (1, blocks), 1)
        column = jnp.zeros((1, blocks), jnp.int32)
        for m in range(1, n_mp + 1):
            column += jnp.where(offsets[m] <= position, 1, 0)
        homes = []
        for i in range(per_shard):
            mine = jnp.where(lists_row[...] == mp * per_shard + i, column, 0)
            homes.append(jnp.minimum(jnp.sum(mine), n_mp - 1))
            home[i] = homes[i]
        start = offsets[mp]
        count = offsets[mp + 1] - start
        shard = []
        for k in range(n_dp):
            shard.append(lists[jnp.minimum(start + k, blocks - 1)] // per_shard)
            slot_shard[k] = shard[k]

        @pl.loop(0, n_mp)
        def _(m):
            chosen = jnp.int32(0)
            for i in range(per_shard):
                chosen = jnp.where(homes[i] == m, i, chosen)
            to_column[m] = chosen
            slot = jnp.int32(0)
            for k in range(n_dp):
                slot = jnp.where((shard[k] == m) & (k < count), k, slot)
            back_slot[m] = slot

    def b0(p):
        c, r = of(p)

        @pl.loop(0, n_mp - 1)
        def _(o):
            to = mp_at(o)
            bsend[c, o, r] = slab[c, to_column[to], r]
            send(bsend.at[c, o, r], arrived[p].at[mp], send_sem.at[S_B], recv_sem.at[R_B + p], {"mp": to})

        arrived[p][mp] = slab[c, to_column[mp], r]

    def c0(p):
        c, r = of(p)
        received(arrived[p].at[pl.ds(1, n_mp - 1)], recv_sem.at[R_B + p])

        @pl.loop(0, n_dp - 1)
        def _(o):
            to = dp_at(o)
            csend[c, o, r] = arrived[p][slot_shard[to]]
            send(csend.at[c, o, r], block.at[c, dp, r], send_sem.at[S_C], recv_sem.at[R_C + p], {"dp": to})

        block[c, dp, r] = arrived[p][slot_shard[dp]]

    def c1(p):
        c, r = of(p)
        received(block.at[c, pl.ds(1, n_dp - 1), r], recv_sem.at[R_C + p])
        if (p + 1) % ROW_PARTS:
            return
        rows_c = block[c].reshape(edge, width)
        product = jnp.dot(rows_c, rv[cols(c), :], preferred_element_type=F32)
        acc[...] = product if c == 0 else acc[...] + product
        part_sq = squares(rows_c.astype(F32))
        sq[3] = part_sq if c == 0 else sq[3] + part_sq

    def q0():
        @pl.loop(1, n_dp)
        def _(o):
            send(sq.at[0], sq_d.at[o], send_sem.at[S_QD], recv_sem.at[R_Q], dp_to(o))

    def q1():
        total = sq[0]
        received(sq_d.at[pl.ds(1, n_dp - 1)], recv_sem.at[R_Q])
        for o in range(1, n_dp):
            total += sq_d[o]
        sq[1] = total
        for o in range(1, NX):
            send(sq.at[1], sq_x.at[o], send_sem.at[S_QX], recv_sem.at[R_Q + 1], x_to(o))

    def q2():
        total = sq[1]
        received(sq_x.at[pl.ds(1, NX - 1)], recv_sem.at[R_Q + 1])
        for o in range(1, NX):
            total += sq_x[o]
        sq[2] = total
        for o in range(1, NZ):
            send(sq.at[2], sq_z.at[o], send_sem.at[S_QZ], recv_sem.at[R_Q + 2], z_to(o))

    def q3():
        total = sq[2]
        received(sq_z.at[pl.ds(1, NZ - 1)], recv_sem.at[R_Q + 2])
        for o in range(1, NZ):
            total += sq_z[o]
        return jnp.sum(total, keepdims=True)

    for d in (4, 5, 3):
        swap(d)
    stages = [a0] + [functools.partial(a_mid, s=s) for s in (1, 2, 3)] + [a4]
    last = pieces - 1
    for turn in range(len(stages) + last // LAG):
        if turn == 4:

            @pl.when(rank < n_mp - 1)
            def _():
                pl.semaphore_wait(entered, n_mp - 1 - rank)

        if 1 <= turn <= 3:
            for d in ((6, 2), (7, 1), (0,))[turn - 1]:
                swap(d)
        for p in range(pieces):
            n = turn - p // LAG
            if 0 <= n < len(stages):
                stages[n](p)
        if turn == 0:
            tables()
    q0()
    q1()
    for p in range(pieces):
        c0(p)
        if p == 0:
            load_r.wait()
        if p == 1:
            q2()
        if p >= 2:
            c1(p - 2)
    c1(last - 1)
    c1(last)

    load_l.wait()
    acc[...] = jnp.dot(lv[...], acc[...].astype(BF16), preferred_element_type=F32)
    precond_sq = sum(squares(acc[:, cols(c)]) for c in range(nc))
    graft = jnp.sqrt(jnp.sum(sq[3], keepdims=True) / area + epsilon) / jnp.sqrt(
        jnp.sum(precond_sq, keepdims=True) / area + epsilon
    )
    clip = max_rms / jnp.sqrt(q3() / cells + epsilon)
    scale = clip * graft

    def d0(p):
        c, r = of(p)
        if p % ROW_PARTS == 0:
            done[c] = (scale * acc[:, cols(c)]).astype(BF16).reshape(n_dp, SLAB, width)

        @pl.loop(0, n_dp - 1)
        def _(o):
            to = dp_at(o)
            send(done.at[c, to, r], rows[p].at[dp], send_sem.at[S_D], recv_sem.at[R_D + p], {"dp": to})

        rows[p][dp] = done[c, dp, r]

    def e0(p):
        c, r = of(p)
        received(rows[p].at[pl.ds(1, n_dp - 1)], recv_sem.at[R_D + p])

        @pl.loop(0, n_mp - 1)
        def _(o):
            to = mp_at(o)
            esend[c, o, r] = rows[p][back_slot[to]]
            send(esend.at[c, o, r], home_in[p].at[mp], send_sem.at[S_E], recv_sem.at[R_E + p], {"mp": to})

        home_in[p][mp] = rows[p][back_slot[mp]]

    def e1(p):
        c, r = of(p)
        received(home_in[p].at[pl.ds(1, n_mp - 1)], recv_sem.at[R_E + p])
        for i in range(per_shard):
            out[i, r, cols(c)] = home_in[p][home[i]]

    for p in range(pieces):
        d0(p)
    for p in range(pieces):
        e0(p)
    for p in range(pieces):
        e1(p)

    all_sent(other, send_sem.at[S_CORE])
    all_sent(red.at[:, 0, 0], send_sem.at[S_HALF])
    all_sent(red.at[:, :, pl.ds(1, 3)], send_sem.at[S_RING])
    all_sent(bsend.at[:, pl.ds(1, n_mp - 1)], send_sem.at[S_B])
    all_sent(csend.at[:, pl.ds(1, n_dp - 1)], send_sem.at[S_C])
    all_sent(csend.at[:, pl.ds(1, n_dp - 1)], send_sem.at[S_D])
    all_sent(esend.at[:, pl.ds(1, n_mp - 1)], send_sem.at[S_E])
    all_sent(sq_d.at[pl.ds(1, n_dp - 1)], send_sem.at[S_QD])
    all_sent(sq_x.at[pl.ds(1, NX - 1)], send_sem.at[S_QX])
    all_sent(sq_z.at[pl.ds(1, NZ - 1)], send_sem.at[S_QZ])


def shards(grad_partials, owner_lists, owner_offsets, left_roots, right_roots):
    _, per_shard, edge, _ = grad_partials.shape
    blocks = owner_lists.shape[0]
    nc = CHUNKS
    width = edge // nc
    piece_rows = SLAB // ROW_PARTS
    pieces = nc * ROW_PARTS
    n_dp, n_mp = 2 * NY, NX * NZ
    g = grad_partials.reshape(per_shard, NY, 2, SLAB, edge)
    dma = pltpu.SemaphoreType.DMA

    small = pl.BlockSpec(memory_space=pltpu.SMEM)
    vmem = pl.BlockSpec(memory_space=pltpu.VMEM)
    large = pl.BlockSpec(memory_space=pltpu.HBM)
    return pl.pallas_call(
        functools.partial(kernel, nc, blocks * edge * edge),
        out_shape=jax.ShapeDtypeStruct((per_shard, SLAB, edge), BF16),
        in_specs=[small, vmem, small, large, large, large],
        out_specs=vmem,
        scratch_shapes=[
            pltpu.VMEM((nc, per_shard, NY, SLAB, width), BF16),
            pltpu.VMEM((nc, per_shard, NY, SLAB, width), BF16),
            pltpu.VMEM((nc, 2, 4, per_shard, SLAB, width), BF16),
            pltpu.VMEM((nc, per_shard, SLAB, width), BF16),
            pltpu.VMEM((nc, n_mp, SLAB, width), BF16),
            [pltpu.VMEM((n_mp, piece_rows, width), BF16)] * pieces,
            pltpu.VMEM((nc, n_dp, SLAB, width), BF16),
            pltpu.VMEM((nc, n_dp, SLAB, width), BF16),
            pltpu.VMEM((nc, n_dp, SLAB, width), BF16),
            [pltpu.VMEM((n_dp, piece_rows, width), BF16)] * pieces,
            pltpu.VMEM((nc, n_mp, SLAB, width), BF16),
            [pltpu.VMEM((n_mp, piece_rows, width), BF16)] * pieces,
            pltpu.VMEM((edge, edge), BF16),
            pltpu.VMEM((edge, edge), BF16),
            pltpu.VMEM((edge, edge), F32),
            pltpu.VMEM((4, 8, 128), F32),
            pltpu.VMEM((n_dp, 8, 128), F32),
            pltpu.VMEM((NX, 8, 128), F32),
            pltpu.VMEM((NZ, 8, 128), F32),
            pltpu.SMEM((n_mp,), jnp.int32),
            pltpu.SMEM((n_dp,), jnp.int32),
            pltpu.SMEM((n_mp,), jnp.int32),
            pltpu.SMEM((per_shard,), jnp.int32),
            dma((nc + 2,)),
            dma((NY,)),
            dma((pieces, 2, 4)),
            dma((10,)),
            dma((4 * pieces + 3,)),
            pltpu.SemaphoreType.REGULAR,
        ],
        compiler_params=pltpu.CompilerParams(
            collective_id=0, has_side_effects=True, vmem_limit_bytes=63 * 1024 * 1024
        ),
    )(owner_lists, owner_lists.reshape(1, blocks), owner_offsets, g, left_roots[0, 0], right_roots[0, 0])


def solution(mesh):
    return jax.shard_map(
        shards,
        mesh=mesh,
        in_specs=(
            P("dp", "mp", None, None),
            P(),
            P(),
            P("mp", "dp", None, None),
            P("mp", "dp", None, None),
        ),
        out_specs=P("mp", "dp", None),
        check_vma=False,
    )
```

```python
import functools

import jax
import jax.numpy as jnp
from jax import lax
from jax.experimental import pallas as pl
from jax.experimental.pallas import tpu as pltpu
from jax.sharding import PartitionSpec as P

MESH = pl.DeviceIdType.MESH
F32 = jnp.float32
BF16 = jnp.bfloat16

epsilon = 1e-06
max_rms = 1.0

CHUNKS = 4
NY, NX, NZ = 8, 4, 8
SLAB = 32
ROW_PARTS = 2
LAG = 8

S_CORE, S_HALF, S_RING, S_B, S_C, S_D, S_E, S_QD, S_QX, S_QZ = range(10)


def kernel(
    nc,
    cells,
    lists,
    lists_row,
    offsets,
    g,
    left,
    right,
    out,
    own,
    other,
    red,
    slab,
    bsend,
    arrived,
    csend,
    block,
    done,
    rows,
    esend,
    home_in,
    lv,
    rv,
    acc,
    sq,
    sq_d,
    sq_x,
    sq_z,
    to_column,
    slot_shard,
    back_slot,
    home,
    sem_in,
    core_r,
    ring_r,
    send_sem,
    recv_sem,
    entered,
):
    per_shard = g.shape[0]
    width = g.shape[-1] // nc
    piece_rows = SLAB // ROW_PARTS
    pieces = nc * ROW_PARTS
    edge = g.shape[-1]
    area = edge * edge
    n_dp, n_mp = 2 * NY, NX * NZ
    R_B, R_C, R_D, R_E, R_Q = 0, pieces, 2 * pieces, 3 * pieces, 4 * pieces
    dp = lax.axis_index("dp")
    mp = lax.axis_index("mp")
    y, core = dp // 2, dp % 2
    x, z = mp // NZ, mp % NZ
    mate = {"dp": y * 2 + (1 - core)}
    y_to = [{"dp": ((y + NY - 1) % NY) * 2 + core}, {"dp": ((y + 1) % NY) * 2 + core}]

    def dp_to(o):
        return {"dp": (dp + o) % n_dp}

    def around(k):
        return 4 + k // 2 - (k % 2) * k

    def mp_at(o):
        return ((x + NX - 1 - o % NX) % NX) * NZ + (z + around(o // NX)) % NZ

    def dp_at(o):
        return ((y + around(o // 2)) % NY) * 2 + (core + 1 - o % 2) % 2

    def x_to(o):
        return {"mp": ((x + o) % NX) * NZ + z}

    def z_to(o):
        return {"mp": x * NZ + (z + o) % NZ}

    def cols(c):
        return pl.ds(c * width, width)

    def of(p):
        return p // ROW_PARTS, pl.ds(p % ROW_PARTS * piece_rows, piece_rows)

    def copy(src, dst, ss, rs, dev):
        return pltpu.make_async_remote_copy(
            src_ref=src, dst_ref=dst, send_sem=ss, recv_sem=rs, device_id=dev, device_id_type=MESH
        )

    def send(*args):
        copy(*args).start()

    def received(dst, rs):
        copy(dst, dst, send_sem.at[0], rs, mate).wait_recv()

    def all_sent(src, ss):
        copy(src, src, ss, recv_sem.at[0], mate).wait_send()

    loads = []
    for c in range(nc):
        load = pltpu.make_async_copy(g.at[:, :, core, :, cols(c)], own.at[c], sem_in.at[c])
        load.start()
        loads.append(load)
    load_r = pltpu.make_async_copy(right, rv, sem_in.at[nc])
    load_r.start()
    load_l = pltpu.make_async_copy(left, lv, sem_in.at[nc + 1])
    load_l.start()

    barrier = pltpu.get_barrier_semaphore()
    rank = z * NX + x

    def ranked(r):
        return {"mp": (r % NX) * NZ + r // NX}

    for near in (*y_to, mate):
        pl.semaphore_signal(barrier, inc=1, device_id=near, device_id_type=MESH)

    @pl.loop(rank + 1, n_mp)
    def _(r):
        pl.semaphore_signal(barrier, inc=1, device_id=ranked(r), device_id_type=MESH)

    pl.semaphore_wait(barrier, 3 + rank)

    @pl.loop(0, rank)
    def _(r):
        pl.semaphore_signal(entered, inc=1, device_id=ranked(r), device_id_type=MESH)

    def swap(d):
        t = (y + d) % NY
        for c in range(nc):
            send(g.at[:, t, 1 - core, :, cols(c)], other.at[c, :, t], send_sem.at[S_CORE], core_r.at[d], mate)

    def mated(p, d):
        t = (y + d) % NY
        if p == 0:
            received(other.at[:, :, t], core_r.at[d])
        return t

    def pair(c, b, t, r):
        return own[c, b, t, r].astype(F32) + other[c, b, t, r].astype(F32)

    whole = pl.ds(0, per_shard)

    def split(p):
        half = per_shard // 2 + p % 2
        return [pl.ds(0, half), pl.ds(half, per_shard - half)]

    def a0(p):
        c, r = of(p)
        if p % ROW_PARTS == 0:
            loads[c].wait()
        t = mated(p, 4)
        own[c, :, t, r] = pair(c, whole, t, r).astype(BF16)
        for way in range(2):
            b = split(p)[way]
            send(own.at[c, b, t, r], red.at[c, way, 0, b, r], send_sem.at[S_HALF], ring_r.at[p, 0], y_to[way])

    def a_mid(p, s):
        c, r = of(p)
        received(red.at[c, 0, 0, :, r] if s == 1 else red.at[c, :, s - 1, :, r], ring_r.at[p, s - 1])
        for way in range(2):
            t = mated(p, 4 + s if way == 0 else 4 - s)
            if s == 1:
                b, rest = split(p)[way], split(p)[1 - way]
                own[c, b, t, r] = (pair(c, b, t, r) + red[c, way, 0, b, r].astype(F32)).astype(BF16)
                own[c, rest, t, r] = pair(c, rest, t, r).astype(BF16)
            else:
                own[c, :, t, r] = (pair(c, whole, t, r) + red[c, way, s - 1, :, r].astype(F32)).astype(BF16)
            send(own.at[c, :, t, r], red.at[c, way, s, :, r], send_sem.at[S_RING], ring_r.at[p, s], y_to[way])

    def squares(v):
        v = (v * v).reshape(-1, 8, v.shape[-1])
        v = jnp.sum(v, axis=0)
        return sum(v[:, i * 128 : (i + 1) * 128] for i in range(v.shape[-1] // 128))

    def a4(p):
        c, r = of(p)
        total = pair(c, whole, mated(p, 0), r)
        received(red.at[c, :, 3, :, r], ring_r.at[p, 3])
        for way in range(2):
            total += red[c, way, 3, :, r].astype(F32)
        total = total.astype(BF16)
        slab[c, :, r] = total
        b0(p)
        part_sq = squares(total.astype(F32))
        sq[0] = part_sq if p == 0 else sq[0] + part_sq

    def tables():
        blocks = lists.shape[0]
        position = lax.broadcasted_iota(jnp.int32, (1, blocks), 1)
        column = jnp.zeros((1, blocks), jnp.int32)
        for m in range(1, n_mp + 1):
            column += jnp.where(offsets[m] <= position, 1, 0)
        homes = []
        for i in range(per_shard):
            mine = jnp.where(lists_row[...] == mp * per_shard + i, column, 0)
            homes.append(jnp.minimum(jnp.sum(mine), n_mp - 1))
            home[i] = homes[i]
        start = offsets[mp]
        count = offsets[mp + 1] - start
        shard = []
        for k in range(n_dp):
            shard.append(lists[jnp.minimum(start + k, blocks - 1)] // per_shard)
            slot_shard[k] = shard[k]

        @pl.loop(0, n_mp)
        def _(m):
            chosen = jnp.int32(0)
            for i in range(per_shard):
                chosen = jnp.where(homes[i] == m, i, chosen)
            to_column[m] = chosen
            slot = jnp.int32(0)
            for k in range(n_dp):
                slot = jnp.where((shard[k] == m) & (k < count), k, slot)
            back_slot[m] = slot

    def b0(p):
        c, r = of(p)

        @pl.loop(0, n_mp - 1)
        def _(o):
            to = mp_at(o)
            bsend[c, o, r] = slab[c, to_column[to], r]
            send(bsend.at[c, o, r], arrived[p].at[mp], send_sem.at[S_B], recv_sem.at[R_B + p], {"mp": to})

        arrived[p][mp] = slab[c, to_column[mp], r]

    def c0(p):
        c, r = of(p)
        received(arrived[p].at[pl.ds(1, n_mp - 1)], recv_sem.at[R_B + p])

        @pl.loop(0, n_dp - 1)
        def _(o):
            to = dp_at(o)
            csend[c, o, r] = arrived[p][slot_shard[to]]
            send(csend.at[c, o, r], block.at[c, dp, r], send_sem.at[S_C], recv_sem.at[R_C + p], {"dp": to})

        block[c, dp, r] = arrived[p][slot_shard[dp]]

    def c1(p):
        c, r = of(p)
        received(block.at[c, pl.ds(1, n_dp - 1), r], recv_sem.at[R_C + p])
        if (p + 1) % ROW_PARTS:
            return
        rows_c = block[c].reshape(edge, width)
        product = jnp.dot(rows_c, rv[cols(c), :], preferred_element_type=F32)
        acc[...] = product if c == 0 else acc[...] + product
        part_sq = squares(rows_c.astype(F32))
        sq[3] = part_sq if c == 0 else sq[3] + part_sq

    def q0():
        @pl.loop(1, n_dp)
        def _(o):
            send(sq.at[0], sq_d.at[o], send_sem.at[S_QD], recv_sem.at[R_Q], dp_to(o))

    def q1():
        total = sq[0]
        received(sq_d.at[pl.ds(1, n_dp - 1)], recv_sem.at[R_Q])
        for o in range(1, n_dp):
            total += sq_d[o]
        sq[1] = total
        for o in range(1, NX):
            send(sq.at[1], sq_x.at[o], send_sem.at[S_QX], recv_sem.at[R_Q + 1], x_to(o))

    def q2():
        total = sq[1]
        received(sq_x.at[pl.ds(1, NX - 1)], recv_sem.at[R_Q + 1])
        for o in range(1, NX):
            total += sq_x[o]
        sq[2] = total
        for o in range(1, NZ):
            send(sq.at[2], sq_z.at[o], send_sem.at[S_QZ], recv_sem.at[R_Q + 2], z_to(o))

    def q3():
        total = sq[2]
        received(sq_z.at[pl.ds(1, NZ - 1)], recv_sem.at[R_Q + 2])
        for o in range(1, NZ):
            total += sq_z[o]
        return jnp.sum(total, keepdims=True)

    for d in (4, 5, 3):
        swap(d)
    stages = [a0] + [functools.partial(a_mid, s=s) for s in (1, 2, 3)] + [a4]
    last = pieces - 1
    for turn in range(len(stages) + last // LAG):
        if turn == 4:

            @pl.when(rank < n_mp - 1)
            def _():
                pl.semaphore_wait(entered, n_mp - 1 - rank)

        if 1 <= turn <= 3:
            for d in ((6, 2), (7, 1), (0,))[turn - 1]:
                swap(d)
        for p in range(pieces):
            n = turn - p // LAG
            if 0 <= n < len(stages):
                stages[n](p)
        if turn == 0:
            tables()
    q0()
    q1()
    for p in range(pieces):
        c0(p)
        if p == 0:
            load_r.wait()
        if p == 1:
            q2()
        if p >= 2:
            c1(p - 2)
    c1(last - 1)
    c1(last)

    load_l.wait()
    acc[...] = jnp.dot(lv[...], acc[...].astype(BF16), preferred_element_type=F32)
    precond_sq = sum(squares(acc[:, cols(c)]) for c in range(nc))
    graft = jnp.sqrt(jnp.sum(sq[3], keepdims=True) / area + epsilon) / jnp.sqrt(
        jnp.sum(precond_sq, keepdims=True) / area + epsilon
    )
    clip = max_rms / jnp.sqrt(q3() / cells + epsilon)
    scale = clip * graft

    def d0(p):
        c, r = of(p)
        if p % ROW_PARTS == 0:
            done[c] = (scale * acc[:, cols(c)]).astype(BF16).reshape(n_dp, SLAB, width)

        @pl.loop(0, n_dp - 1)
        def _(o):
            to = dp_at(o)
            send(done.at[c, to, r], rows[p].at[dp], send_sem.at[S_D], recv_sem.at[R_D + p], {"dp": to})

        rows[p][dp] = done[c, dp, r]

    def e0(p):
        c, r = of(p)
        received(rows[p].at[pl.ds(1, n_dp - 1)], recv_sem.at[R_D + p])

        @pl.loop(0, n_mp - 1)
        def _(o):
            to = mp_at(o)
            esend[c, o, r] = rows[p][back_slot[to]]
            send(esend.at[c, o, r], home_in[p].at[mp], send_sem.at[S_E], recv_sem.at[R_E + p], {"mp": to})

        home_in[p][mp] = rows[p][back_slot[mp]]

    def e1(p):
        c, r = of(p)
        received(home_in[p].at[pl.ds(1, n_mp - 1)], recv_sem.at[R_E + p])
        for i in range(per_shard):
            out[i, r, cols(c)] = home_in[p][home[i]]

    for p in range(pieces):
        d0(p)
    for p in range(pieces):
        e0(p)
    for p in range(pieces):
        e1(p)

    all_sent(other, send_sem.at[S_CORE])
    all_sent(red.at[:, 0, 0], send_sem.at[S_HALF])
    all_sent(red.at[:, :, pl.ds(1, 3)], send_sem.at[S_RING])
    all_sent(bsend.at[:, pl.ds(1, n_mp - 1)], send_sem.at[S_B])
    all_sent(csend.at[:, pl.ds(1, n_dp - 1)], send_sem.at[S_C])
    all_sent(csend.at[:, pl.ds(1, n_dp - 1)], send_sem.at[S_D])
    all_sent(esend.at[:, pl.ds(1, n_mp - 1)], send_sem.at[S_E])
    all_sent(sq_d.at[pl.ds(1, n_dp - 1)], send_sem.at[S_QD])
    all_sent(sq_x.at[pl.ds(1, NX - 1)], send_sem.at[S_QX])
    all_sent(sq_z.at[pl.ds(1, NZ - 1)], send_sem.at[S_QZ])


def shards(grad_partials, owner_lists, owner_offsets, left_roots, right_roots):
    _, per_shard, edge, _ = grad_partials.shape
    blocks = owner_lists.shape[0]
    nc = CHUNKS
    width = edge // nc
    piece_rows = SLAB // ROW_PARTS
    pieces = nc * ROW_PARTS
    n_dp, n_mp = 2 * NY, NX * NZ
    g = grad_partials.reshape(per_shard, NY, 2, SLAB, edge)
    dma = pltpu.SemaphoreType.DMA

    small = pl.BlockSpec(memory_space=pltpu.SMEM)
    vmem = pl.BlockSpec(memory_space=pltpu.VMEM)
    large = pl.BlockSpec(memory_space=pltpu.HBM)
    return pl.pallas_call(
        functools.partial(kernel, nc, blocks * edge * edge),
        out_shape=jax.ShapeDtypeStruct((per_shard, SLAB, edge), BF16),
        in_specs=[small, vmem, small, large, large, large],
        out_specs=vmem,
        scratch_shapes=[
            pltpu.VMEM((nc, per_shard, NY, SLAB, width), BF16),
            pltpu.VMEM((nc, per_shard, NY, SLAB, width), BF16),
            pltpu.VMEM((nc, 2, 4, per_shard, SLAB, width), BF16),
            pltpu.VMEM((nc, per_shard, SLAB, width), BF16),
            pltpu.VMEM((nc, n_mp, SLAB, width), BF16),
            [pltpu.VMEM((n_mp, piece_rows, width), BF16)] * pieces,
            pltpu.VMEM((nc, n_dp, SLAB, width), BF16),
            pltpu.VMEM((nc, n_dp, SLAB, width), BF16),
            pltpu.VMEM((nc, n_dp, SLAB, width), BF16),
            [pltpu.VMEM((n_dp, piece_rows, width), BF16)] * pieces,
            pltpu.VMEM((nc, n_mp, SLAB, width), BF16),
            [pltpu.VMEM((n_mp, piece_rows, width), BF16)] * pieces,
            pltpu.VMEM((edge, edge), BF16),
            pltpu.VMEM((edge, edge), BF16),
            pltpu.VMEM((edge, edge), F32),
            pltpu.VMEM((4, 8, 128), F32),
            pltpu.VMEM((n_dp, 8, 128), F32),
            pltpu.VMEM((NX, 8, 128), F32),
            pltpu.VMEM((NZ, 8, 128), F32),
            pltpu.SMEM((n_mp,), jnp.int32),
            pltpu.SMEM((n_dp,), jnp.int32),
            pltpu.SMEM((n_mp,), jnp.int32),
            pltpu.SMEM((per_shard,), jnp.int32),
            dma((nc + 2,)),
            dma((NY,)),
            dma((pieces, 4)),
            dma((10,)),
            dma((4 * pieces + 3,)),
            pltpu.SemaphoreType.REGULAR,
        ],
        compiler_params=pltpu.CompilerParams(
            collective_id=0, has_side_effects=True, vmem_limit_bytes=63 * 1024 * 1024
        ),
    )(owner_lists, owner_lists.reshape(1, blocks), owner_offsets, g, left_roots[0, 0], right_roots[0, 0])


def solution(mesh):
    return jax.shard_map(
        shards,
        mesh=mesh,
        in_specs=(
            P("dp", "mp", None, None),
            P(),
            P(),
            P("mp", "dp", None, None),
            P("mp", "dp", None, None),
        ),
        out_specs=P("mp", "dp", None),
        check_vma=False,
    )
```
